32 devices in a mesh: front: 2 (over core), row: 8 (over z, x), col: 2 (over y).
Axes of the slice: x: 2, y: 2, z: 4, core: 2. Of those that a mesh axis runs over, the one named last changes fastest.
Arguments:
- window: bfloat16 [2, 8192, 1024], P('front', 'row', 'col'), may hold values from -4 to 7.3, as said below
- children: bfloat16 [512, 128, 128], P(('front', 'row', 'col')), may hold values from -4 to 4
- routes: int32 [512, 1], P(('front', 'row', 'col')), may hold values from 0 to 15; in each aligned block of 16 rows (0 to 15, 16 to 31, ...) at most 2 rows name the same one
- slots: int32 [512], P(('front', 'row', 'col')), may hold values from 0 to 15
- pattern: int32 [2, 16, 2], P('front', 'row', 'col'), may hold values 0 or 1
Outputs:
- factored: bfloat16 [2, 8192, 1024], P('front', 'row', 'col')
The draws below stay inside these ranges and needn't reach their ends.
Inputs may be any that keep to these rules, and one draw needn't show every extreme that they name: `routes`: among the rows of one device (aligned blocks of 16 rows) no owner group is named by more than 2 rows, a bound that some block reaches. `slots`: child blocks land only below the first tile row of each owner's part. `window`: each front's rows and columns [0, 512) hold a symmetric positive definite tile.
All inputs are finite; a program needn't handle non-finite values. No bound on the sum of `pattern` on one device may be relied on, other than what follows from the above.
Results may differ from the reference program's by a relative error of at most 0.0056.
Values may be sent and summed in bfloat16 or wider, within the bound.
A program may use at most 64 MiB of HBM per device.

```python
import math
import jax
import jax.numpy as jnp
import numpy as np
from jax import lax

TILE = 512
SB = 128
TR_DEV = 2
CAP = 2
P_SIZE = 8192
NT = 16
CB = 16
SLOTS = 16
N_FRONT = 2
N_ROW = 8
N_COL = 2


def draw_window(key, part):
    keys = jax.random.split(key, 4)
    shape = (N_FRONT, P_SIZE, N_COL * TILE)
    base = jax.random.truncated_normal(keys[0], -4.0, 4.0, shape, jnp.float32)
    position = jnp.arange(TILE, dtype=jnp.float32)
    distance = jnp.abs(position[:, None] - position[None, :])
    gains = jax.random.uniform(keys[1], (N_FRONT, TILE), jnp.float32, 0.5, 1.5)
    noise = jax.random.uniform(keys[2], (N_FRONT, TILE, TILE), jnp.float32, -0.004, 0.004)
    noise = noise + jnp.swapaxes(noise, 1, 2)
    signs = jax.random.rademacher(keys[3], (N_FRONT, TILE, TILE), jnp.float32)
    upper_signs = jnp.triu(signs, 1)
    sign_term = 0.03 * (upper_signs + jnp.swapaxes(upper_signs, 1, 2))
    pivot = gains[:, :, None] * gains[:, None, :] * jnp.exp(-distance / 16.0)[None] + noise + sign_term + 4.9 * jnp.eye(TILE, dtype=jnp.float32)[None]
    base = base.at[:, :TILE, :TILE].set(pivot)
    return base.astype(jnp.bfloat16)


def touch_ends(drawn, stream_key, least, high):
    shape = drawn.shape
    index_at = [jax.random.randint(jax.random.fold_in(stream_key, axis), (), 0, shape[axis]) for axis in range(len(shape))]
    drawn = drawn.at[tuple(index_at)].set(least)
    longest = shape.index(max(shape))
    index_at[longest] = (index_at[longest] + 1) % shape[longest]
    return drawn.at[tuple(index_at)].set(high)


def level_of(own_key, shape, cuts, smallest, largest):
    def one(axis_at, shards_of):
        draws = jax.random.uniform(jax.random.fold_in(jax.random.fold_in(own_key, 6), axis_at), (shards_of,), jnp.float32, smallest / len(cuts), largest / len(cuts))
        return jnp.repeat(jnp.exp(draws), shape[axis_at] // shards_of).reshape((-1,) + (1,) * (len(shape) - axis_at - 1))

    loudness = one(*cuts[0])
    for cut in cuts[1:]:
        loudness = loudness * one(*cut)
    return loudness


def routed_block(key, own, number, rows, number_of, top, reach, skew):
    order = jax.random.permutation(key, number_of)
    crowded, usual = load_shares(number_of, rows * top, reach, skew, True), load_shares(number_of, rows * top, reach, skew, False)
    places = jnp.arange(number_of)

    def named(tallies, turn):
        used = int((tallies > 0).sum())
        fixed = max(1, used // 4)
        shifted = fixed + (places - fixed + turn * (used - fixed)) % max(1, number_of - fixed)
        return jnp.zeros((number_of,), jnp.int32).at[order[jnp.where(places < fixed, places, shifted)]].set(jnp.asarray(tallies, jnp.int32))

    tallies = jnp.where(number % 4 == 0, named(crowded, number // 4), named(usual, number - number // 4 - 1))
    mixed = jax.random.permutation(jax.random.fold_in(own, 3), number_of)
    giver, taker = mixed[0:number_of // 2 * 2:2], mixed[1:number_of // 2 * 2:2]
    margin = jnp.minimum(tallies[giver] - 1, reach - tallies[taker]) // 2
    margin = jnp.where((giver == order[0]) | (taker == order[0]) | (tallies[taker] == 0), 0, jnp.maximum(margin, 0))
    shifted = jax.random.randint(jax.random.fold_in(own, 4), (number_of // 2,), 0, 1 << 20) % (margin + 1)
    tallies = tallies.at[giver].add(-shifted).at[taker].add(shifted)
    labels = jnp.searchsorted(jnp.cumsum(tallies), jnp.arange(rows * top), side="right").astype(jnp.int32)
    table = labels.reshape(top, rows).T
    table = table[jax.random.permutation(jax.random.fold_in(own, 1), rows)]
    turn = jax.random.randint(jax.random.fold_in(own, 2), (rows, 1), 0, top)
    return jnp.take_along_axis(table, (jnp.arange(top)[None, :] + turn) % top, axis=1)


def load_shares(count, total, reach, skew, full):
    weights = [(1 << 20) // math.isqrt(grade ** skew) + 1 for grade in range(1, count + 1)]
    largest = reach if full else min(reach, max(-(-total // count), total * weights[0] // sum(weights)))
    least = 1 if total - largest >= count - 1 else 0
    holding, rest = [largest] + [least] * (count - 1), total - largest - least * (count - 1)
    while rest > 0:
        movable = [i for i in range(1, count) if holding[i] < largest] or [i for i in range(1, count) if holding[i] < reach]
        whole, remaining = sum([weights[i] for i in movable]), rest
        for i in movable:
            extra = min(reach - holding[i], max(1, remaining * weights[i] // whole), rest)
            holding[i] = holding[i] + extra
            rest = rest - extra
    return np.array(holding)


def scatter_about(rng, dims, width, limit, pieces=(), held_as=jnp.bfloat16):
    values = width * jax.random.normal(rng, dims, jnp.float32)
    if pieces:
        values = values * level_of(rng, dims, pieces, -0.22, 0.18)
    return jnp.clip(values, -limit, limit).astype(held_as)


def setup_inputs(seed: int = 0) -> dict:
    key_list = jax.random.split(jax.random.key(seed), 6)
    window = draw_window(jax.random.fold_in(key_list[5], 71), 0)
    children = scatter_about(key_list[1], (N_FRONT * N_ROW * N_COL * CB, SB, SB), 1.0, 4.0, ((0, 32),))
    routes_keys = jax.random.split(jax.random.fold_in(key_list[2], 1), (N_FRONT * N_ROW * N_COL * CB) // CB)
    routes_turns = jax.random.permutation(jax.random.fold_in(key_list[2], 3), (N_FRONT * N_ROW * N_COL * CB) // CB)
    routes = jax.vmap(lambda own, number: routed_block(jax.random.fold_in(key_list[2], 2), own, number, CB, N_FRONT * N_ROW, 1, CAP, 2))(routes_keys, routes_turns).reshape((N_FRONT * N_ROW * N_COL * CB, 1))
    slots = touch_ends(jax.random.randint(key_list[3], (N_FRONT * N_ROW * N_COL * CB,), 0, SLOTS), jax.random.fold_in(key_list[3], 1), 0, SLOTS - 1).astype(jnp.int32)
    pattern = touch_ends((jax.random.randint(key_list[4], (N_FRONT, NT, N_COL), 0, 3) < 2).astype(jnp.int32), jax.random.fold_in(key_list[4], 1), 0, 1)
    return dict(window=window, children=children, routes=routes, slots=slots, pattern=pattern)


def reference(window, children, routes, slots, pattern):
    side = TILE // SB
    row_blocks = P_SIZE // SB
    col_blocks = N_COL * side
    count = children.shape[0]
    owner_dev = jnp.arange(count, dtype=jnp.int32) // CB
    sender_col = owner_dev % N_COL
    target = routes[:, 0]
    target_front = target // N_ROW
    target_row = target % N_ROW
    block_row = target_row * (TR_DEV * side) + side + slots // side
    block_col = sender_col * side + slots % side

    def one_front(items):
        front_id, win, mask = items
        grid = win.astype(jnp.float32).reshape(row_blocks, SB, col_blocks, SB).transpose(0, 2, 1, 3)
        rows = jnp.where(target_front == front_id, block_row, row_blocks).astype(jnp.int32)
        grid = grid.at[rows, block_col].add(children.astype(jnp.float32), mode='drop')
        assembled = grid.transpose(0, 2, 1, 3).reshape(P_SIZE, N_COL * TILE)
        panel = assembled[:, :TILE]
        chol = jnp.linalg.cholesky(panel[:TILE])
        lower = jax.scipy.linalg.solve_triangular(chol, panel.T, lower=True).T.astype(jnp.bfloat16)
        lower_f = lower.astype(jnp.float32)
        update = jnp.dot(lower_f, lower_f[:N_COL * TILE].T, precision=lax.Precision.HIGHEST)
        live = jnp.repeat(jnp.repeat(mask.astype(jnp.float32), TILE, axis=0), TILE, axis=1)
        result = (assembled - live * update).astype(jnp.bfloat16)
        return result.at[:, :TILE].set(lower)
    fronts = jnp.arange(N_FRONT, dtype=jnp.int32)
    return lax.map(one_front, (fronts, window, pattern))
```

```python
import functools

import jax
import jax.numpy as jnp
from jax import lax
from jax.experimental import pallas as pl
from jax.experimental.pallas import tpu as pltpu
from jax.sharding import PartitionSpec as P

TILE = 512
SB = 128
CAP = 2
SUB = 32
MESH = pl.DeviceIdType.MESH
HIGH = lax.Precision.HIGHEST


def inner_rows(rows):
    inner = 1
    while inner * inner * 4 <= rows:
        inner *= 2
    return inner


def row_tree(f, rel, base, c, rows):
    inner = inner_rows(rows)
    edges = []
    for k in range(1, inner):
        edges.append((rel == 0, (f, lax.rem(base + k, rows), c)))
    edges.append((rel + inner < rows, (f, lax.rem(base + rel + inner, rows), c)))
    return edges


def row_parent(f, rel, base, c, rows):
    inner = inner_rows(rows)
    up = jnp.where(rel < inner, 0, rel - inner)
    return (f, lax.rem(base + up, rows), c)


def remote(src, dst, send, recv, device):
    return pltpu.make_async_remote_copy(
        src_ref=src, dst_ref=dst, send_sem=send, recv_sem=recv, device_id=device, device_id_type=MESH
    )


def exchange_kernel(
    fronts, rows, cols, index, tagrows, children, window, incoming, pivot, top, outgoing,
    send, recv, pivot_send, pivot_recv, top_send, top_recv, local,
):
    f, r, c = lax.axis_index("front"), lax.axis_index("row"), lax.axis_index("col")
    groups = fronts * rows
    me = f * rows + r
    chunk = TILE // 4
    tree = [((r == 0) & (c == 0), (f, 0, k)) for k in range(1, cols)] + row_tree(f, r, 0, c, rows)
    root = (r == 0) & (c == 0)

    barrier = pltpu.get_barrier_semaphore()

    def greet(k, carry):
        g = lax.rem(me + k, groups)
        pl.semaphore_signal(barrier, inc=1, device_id=(g // rows, lax.rem(g, rows), c), device_id_type=MESH)
        return carry

    lax.fori_loop(1, groups, greet, 0)
    for k in range(1, cols):
        pl.semaphore_signal(barrier, inc=1, device_id=(f, r, lax.rem(c + k, cols)), device_id_type=MESH)

    def pack(g, carry):
        for j in range(CAP):
            outgoing[g, j * SB : (j + 1) * SB, :] = children[index[g * CAP + j]]
        outgoing[g, CAP * SB :, :] = tagrows[g]
        return carry

    lax.fori_loop(0, groups, pack, 0)
    pl.semaphore_wait(barrier, groups - 1 + cols - 1)

    def part(ref, i):
        return ref.at[pl.ds(i * chunk, chunk), pl.ds(0, (i + 1) * chunk)]

    def hand_on(i, source):
        for e, (live, device) in enumerate(tree):
            @pl.when(live)
            def _():
                remote(part(source, i), part(pivot, i), pivot_send.at[e, i], pivot_recv.at[i], device).start()

    @pl.when(root)
    def _():
        for i in range(4):
            hand_on(i, window)

    @pl.when(c == 0)
    def _():
        for k in range(1, cols):
            remote(window.at[pl.ds(0, TILE), :], top, top_send.at[k], top_recv, (f, r, k)).start()

    def ship(k):
        g = lax.rem(me + k, groups)
        return remote(outgoing.at[g], incoming.at[me], send.at[k], recv.at[k], (g // rows, lax.rem(g, rows), c))

    def land(k):
        g = lax.rem(me + groups - k, groups)
        return remote(outgoing.at[g], incoming.at[g], send.at[k], recv.at[k], (g // rows, lax.rem(g, rows), c))

    def start(k, carry):
        ship(k).start()
        return carry

    lax.fori_loop(1, groups, start, 0)
    own = pltpu.make_async_copy(outgoing.at[me], incoming.at[me], local.at[0])
    own.start()

    @pl.when(root)
    def _():
        for i in range(4):
            copy = pltpu.make_async_copy(part(window, i), part(pivot, i), local.at[1 + i])
            copy.start()
        for i in range(4):
            pltpu.make_async_copy(part(window, i), part(pivot, i), local.at[1 + i]).wait()

    @pl.when(jnp.logical_not(root))
    def _():
        for i in range(4):
            remote(part(window, i), part(pivot, i), pivot_send.at[0, i], pivot_recv.at[i], (f, 0, 0)).wait_recv()
            hand_on(i, pivot)

    def drain(k, carry):
        land(k).wait_recv()
        ship(k).wait_send()
        return carry

    lax.fori_loop(1, groups, drain, 0)
    own.wait()
    for e, (live, device) in enumerate(tree):
        @pl.when(live)
        def _():
            for i in range(4):
                remote(part(window, i), part(pivot, i), pivot_send.at[e, i], pivot_recv.at[i], device).wait_send()

    @pl.when(c == 0)
    def _():
        for k in range(1, cols):
            remote(window.at[pl.ds(0, TILE), :], top, top_send.at[k], top_recv, (f, r, k)).wait_send()

    @pl.when(c > 0)
    def _():
        remote(window.at[pl.ds(0, TILE), :], top, top_send.at[0], top_recv, (f, r, 0)).wait_recv()


def dot(a, b, dims=(((1,), (0,)), ((), ()))):
    return lax.dot_general(a, b, dims, precision=HIGH, preferred_element_type=jnp.float32)


def invert_small(block):
    row = lax.broadcasted_iota(jnp.int32, (SUB, SB), 0)
    lane = lax.broadcasted_iota(jnp.int32, (SUB, SB), 1)
    work = jnp.where(lane < SUB, block, (lane == row + 2 * SUB).astype(jnp.float32))
    for k in range(SUB):
        column = jnp.broadcast_to(work[:, k : k + 1], (SUB, SB))
        scale = lax.rsqrt(jnp.broadcast_to(column[k : k + 1, :], (SUB, SB)))
        line = jnp.broadcast_to(work[k : k + 1, :], (SUB, SB)) * scale
        work = jnp.where(row > k, work - column * scale * line, jnp.where(row == k, line, work))
    return work[:, 2 * SUB : 3 * SUB]


def factor_block(b, a, u, inv, ext):
    at = b * SB
    width = TILE - at
    ext[:, :width] = a[at : at + SB, at:]
    ext[:, width : width + SB] = (
        lax.broadcasted_iota(jnp.int32, (SB, SB), 0) == lax.broadcasted_iota(jnp.int32, (SB, SB), 1)
    ).astype(jnp.float32)
    steps = SB // SUB
    for s in range(steps):
        lo = s * SUB
        line = ext[lo : lo + SUB, : width + SB]
        diagonal = line[:, :SB]
        if s:
            diagonal = pltpu.roll(diagonal, SB - lo, 1)
        small = invert_small(diagonal)
        new = dot(small, line)
        lane = lax.broadcasted_iota(jnp.int32, new.shape, 1)
        new = jnp.where(lane < lo, 0.0, new)
        ext[lo : lo + SUB, : width + SB] = new
        if s + 1 < steps:
            left = dot(new[:, :SB], new, (((0,), (0,)), ((), ())))
            ext[lo + SUB :, : width + SB] -= left[lo + SUB :]
    u[at : at + SB, at:] = ext[:, :width]
    inv[b] = ext[:, width : width + SB]
    if b < TILE // SB - 1:
        rest = ext[:, SB:width]
        a[at + SB :, at + SB :] -= dot(rest, rest, (((0,), (0,)), ((), ())))


def symmetric(pivot, a):
    for i in range(TILE // SB):
        for j in range(i + 1):
            piece = pivot[i * SB : (i + 1) * SB, j * SB : (j + 1) * SB].astype(jnp.float32)
            a[i * SB : (i + 1) * SB, j * SB : (j + 1) * SB] = piece
            if i > j:
                a[j * SB : (j + 1) * SB, i * SB : (i + 1) * SB] = piece.T


def assemble_kernel(marks, window, incoming, pivot, acc, bottom, u, inv, a, ext):
    groups = incoming.shape[0]
    side = TILE // SB
    acc[...] = window[TILE:, :].astype(jnp.float32)

    def add(p, carry):
        mark = marks[p]

        @pl.when(mark > 0)
        def _():
            slot = mark - 1
            high = pl.ds(pl.multiple_of(slot // side * SB, SB), SB)
            wide = pl.ds(pl.multiple_of(slot % side * SB, SB), SB)
            block = incoming[p // CAP, pl.ds(pl.multiple_of(p % CAP * SB, SB), SB), :]
            acc[high, wide] += block.astype(jnp.float32)

        return carry

    lax.fori_loop(0, groups * CAP, add, 0)
    bottom[...] = acc[...].astype(jnp.bfloat16)
    symmetric(pivot, a)
    u[...] = jnp.zeros_like(u)
    for b in range(TILE // SB):
        factor_block(b, a, u, inv, ext)


def solve_rows(panel, u, inv, out):
    done = []
    for j in range(TILE // SB):
        part = panel[:, j * SB : (j + 1) * SB]
        for k in range(j):
            part = part - dot(done[k], u[k * SB : (k + 1) * SB, j * SB : (j + 1) * SB])
        done.append(dot(part, inv[j], (((1,), (1,)), ((), ()))))
        out[:, j * SB : (j + 1) * SB] = done[-1].astype(jnp.bfloat16)


def finish_kernel(
    rows, cols, pattern, window, top, acc, bottom, u, inv, out, panel, partner, lower, mate,
    panel_send, panel_recv, mate_send, mate_recv,
):
    f, r, c = lax.axis_index("front"), lax.axis_index("row"), lax.axis_index("col")
    tiles = window.shape[0] // TILE
    owner, within = c // tiles, lax.rem(c, tiles)
    rel = lax.rem(r - owner + rows, rows)
    chunk = TILE // 4
    tree = row_tree(f, rel, owner, c, rows)
    parent = row_parent(f, rel, owner, c, rows)

    barrier = pltpu.get_barrier_semaphore()
    for k in range(1, cols):
        pl.semaphore_signal(barrier, inc=1, device_id=(f, r, lax.rem(c + k, cols)), device_id_type=MESH)
    for k in range(1, rows):
        pl.semaphore_signal(barrier, inc=1, device_id=(f, lax.rem(r + k, rows), c), device_id_type=MESH)
    pl.semaphore_wait(barrier, rows - 1 + cols - 1)

    def rows_of(ref, i):
        return ref.at[pl.ds(i * chunk, chunk), :]

    def send_panel(k, i):
        return remote(rows_of(bottom, i), rows_of(panel, i), panel_send.at[k, i], panel_recv.at[i], (f, r, k))

    def give(e, device, source, i):
        return remote(rows_of(source, i), rows_of(partner, i), mate_send.at[e, i], mate_recv.at[i], device)

    def hand_on(source, i):
        for e, (live, device) in enumerate(tree):
            @pl.when(live)
            def _():
                give(e, device, source, i).start()

    @pl.when(c == 0)
    def _():
        for i in range(4):
            for k in range(1, cols):
                send_panel(k, i).start()
        lower[:TILE, :] = window[:TILE, :].astype(jnp.float32)
        lower[TILE:, :] = acc[...]
        solve_rows(lower, u, inv, out)
        for i in range(4):
            for k in range(1, cols):
                send_panel(k, i).wait_send()

    @pl.when(c > 0)
    def _():
        for i in range(4):
            send_panel(0, i).wait_recv()

            @pl.when((rel == 0) & (within != 0))
            def _():
                hand_on(panel, i)
                partner[i * chunk : (i + 1) * chunk, :] = panel[i * chunk : (i + 1) * chunk, :]

            @pl.when((rel == 0) & (within == 0))
            def _():
                hand_on(top, i)
                partner[i * chunk : (i + 1) * chunk, :] = top[i * chunk : (i + 1) * chunk, :]

        lower[:TILE, :] = top[...].astype(jnp.float32)
        lower[TILE:, :] = panel[...].astype(jnp.float32)
        solve_rows(lower, u, inv, out)

        @pl.when(rel > 0)
        def _():
            for i in range(4):
                give(0, parent, partner, i).wait_recv()
                hand_on(partner, i)

        solve_rows(partner[...].astype(jnp.float32), u, inv, mate)
        for t in range(tiles):
            product = lax.dot_general(
                out[t * TILE : (t + 1) * TILE, :], mate[...], (((1,), (1,)), ((), ())),
                preferred_element_type=jnp.float32,
            )
            base = window[:TILE, :].astype(jnp.float32) if t == 0 else acc[(t - 1) * TILE : t * TILE, :]
            live = pattern[t].astype(jnp.float32)
            out[t * TILE : (t + 1) * TILE, :] = (base - live * product).astype(jnp.bfloat16)
        for e, (live, device) in enumerate(tree):
            @pl.when(live)
            def _():
                for i in range(4):
                    give(e, device, partner, i).wait_send()


def spec(space):
    return pl.BlockSpec(memory_space=space)


def shards(window, children, routes, slots, pattern):
    fronts, rows, cols = lax.axis_size("front"), lax.axis_size("row"), lax.axis_size("col")
    groups = fronts * rows
    count = children.shape[0]
    window = window[0]
    height = window.shape[0]
    target = routes[:, 0]
    earlier = (lax.broadcasted_iota(jnp.int32, (count, count), 0) > lax.broadcasted_iota(jnp.int32, (count, count), 1))
    rank = jnp.sum((earlier & (target[:, None] == target[None, :])).astype(jnp.int32), axis=1)
    place = target * CAP + rank
    hit = lax.broadcasted_iota(jnp.int32, (groups * CAP, count), 0) == place[None, :]
    index = jnp.sum(jnp.where(hit, lax.broadcasted_iota(jnp.int32, hit.shape, 1), 0), axis=1)
    tag = jnp.sum(jnp.where(hit, slots[None, :] + 1, 0), axis=1)
    tagrows = jnp.zeros((groups, 16, SB), jnp.float32) + jnp.pad(
        tag.reshape(groups, CAP).astype(jnp.float32), ((0, 0), (0, SB - CAP))
    )[:, None, :]
    tagrows = tagrows.astype(jnp.bfloat16)
    deep = CAP * SB + 16
    edges = cols - 1 + inner_rows(rows)
    vmem, smem, hbm = pltpu.VMEM, pltpu.SMEM, pl.ANY
    dma = pltpu.SemaphoreType.DMA
    incoming, pivot, top = pl.pallas_call(
        functools.partial(exchange_kernel, fronts, rows, cols),
        out_shape=(
            jax.ShapeDtypeStruct((groups, deep, SB), jnp.bfloat16),
            jax.ShapeDtypeStruct((TILE, TILE), jnp.bfloat16),
            jax.ShapeDtypeStruct((TILE, TILE), jnp.bfloat16),
        ),
        in_specs=[spec(smem), spec(vmem), spec(vmem), spec(hbm)],
        out_specs=(spec(hbm), spec(hbm), spec(hbm)),
        scratch_shapes=[
            vmem((groups, deep, SB), jnp.bfloat16),
            dma((groups,)), dma((groups,)), dma((edges, 4)), dma((4,)), dma((cols,)), dma(()), dma((5,)),
        ],
        compiler_params=pltpu.CompilerParams(
            collective_id=0, has_side_effects=True, vmem_limit_bytes=32 << 20
        ),
    )(index, tagrows, children, window)
    marks = incoming[:, CAP * SB, :CAP].astype(jnp.int32).reshape(groups * CAP)
    acc, bottom, u, inv = pl.pallas_call(
        assemble_kernel,
        out_shape=(
            jax.ShapeDtypeStruct((height - TILE, TILE), jnp.float32),
            jax.ShapeDtypeStruct((height - TILE, TILE), jnp.bfloat16),
            jax.ShapeDtypeStruct((TILE, TILE), jnp.float32),
            jax.ShapeDtypeStruct((TILE // SB, SB, SB), jnp.float32),
        ),
        in_specs=[spec(smem), spec(vmem), spec(vmem), spec(vmem)],
        out_specs=(spec(vmem),) * 4,
        scratch_shapes=[vmem((TILE, TILE), jnp.float32), vmem((SB, TILE + SB), jnp.float32)],
        compiler_params=pltpu.CompilerParams(vmem_limit_bytes=48 << 20),
    )(marks, window, incoming, pivot)
    result = pl.pallas_call(
        functools.partial(finish_kernel, rows, cols),
        out_shape=jax.ShapeDtypeStruct((height, TILE), jnp.bfloat16),
        in_specs=[spec(smem)] + [spec(vmem)] * 6,
        out_specs=spec(vmem),
        scratch_shapes=[
            vmem((TILE, TILE), jnp.bfloat16), vmem((TILE, TILE), jnp.bfloat16),
            vmem((height, TILE), jnp.float32), vmem((TILE, TILE), jnp.bfloat16),
            dma((cols, 4)), dma((4,)), dma((inner_rows(rows), 4)), dma((4,)),
        ],
        compiler_params=pltpu.CompilerParams(
            collective_id=1, has_side_effects=True, vmem_limit_bytes=48 << 20
        ),
    )(pattern[0, :, 0], window, top, acc, bottom, u, inv)
    return result[None]


def solution(mesh):
    placed = (
        P("front", "row", "col"),
        P(("front", "row", "col"), None, None),
        P(("front", "row", "col"), None),
        P(("front", "row", "col")),
        P("front", "row", "col"),
    )
    return jax.shard_map(
        shards, mesh=mesh, in_specs=placed, out_specs=P("front", "row", "col"), check_vma=False
    )
```

```python
import functools

import jax
import jax.numpy as jnp
from jax import lax
from jax.experimental import pallas as pl
from jax.experimental.pallas import tpu as pltpu
from jax.sharding import PartitionSpec as P

TILE = 512
SB = 128
CAP = 2
SUB = 32
GROUP = 8
HALF = 2
MESH = pl.DeviceIdType.MESH
HIGH = lax.Precision.HIGHEST


def inner_rows(rows):
    inner = 1
    while inner * inner * 4 <= rows:
        inner *= 2
    return inner


def row_tree(f, rel, base, c, rows):
    inner = inner_rows(rows)
    edges = []
    for k in range(1, inner):
        edges.append((rel == 0, (f, lax.rem(base + k, rows), c)))
    edges.append((rel + inner < rows, (f, lax.rem(base + rel + inner, rows), c)))
    return edges


def row_parent(f, rel, base, c, rows):
    inner = inner_rows(rows)
    up = jnp.where(rel < inner, 0, rel - inner)
    return (f, lax.rem(base + up, rows), c)


def remote(src, dst, send, recv, device):
    return pltpu.make_async_remote_copy(
        src_ref=src, dst_ref=dst, send_sem=send, recv_sem=recv, device_id=device, device_id_type=MESH
    )


def exchange_kernel(
    fronts, rows, cols, index, tagrows, children, window, incoming, top, rest, u, inv, pivot, a, ext, outgoing,
    send, recv, pivot_send, pivot_recv, top_send, top_recv, local,
):
    f, r, c = lax.axis_index("front"), lax.axis_index("row"), lax.axis_index("col")
    groups = fronts * rows
    me = f * rows + r
    chunk = TILE // 4
    tree = [((r == 0) & (c == 0), (f, 0, k)) for k in range(1, cols)] + row_tree(f, r, 0, c, rows)
    root = (r == 0) & (c == 0)

    barrier = pltpu.get_barrier_semaphore()

    def greet(k, carry):
        g = lax.rem(me + k, groups)
        pl.semaphore_signal(barrier, inc=1, device_id=(g // rows, lax.rem(g, rows), c), device_id_type=MESH)
        return carry

    lax.fori_loop(1, groups, greet, 0)
    for k in range(1, cols):
        pl.semaphore_signal(barrier, inc=1, device_id=(f, r, lax.rem(c + k, cols)), device_id_type=MESH)

    def pack(g, carry):
        for j in range(CAP):
            outgoing[g, j * SB : (j + 1) * SB, :] = children[index[g * CAP + j]]
        outgoing[g, CAP * SB :, :] = tagrows[g]
        return carry

    lax.fori_loop(0, groups, pack, 0)
    pl.semaphore_wait(barrier, groups - 1 + cols - 1)

    def part(ref, i):
        return ref.at[pl.ds(i * chunk, chunk), pl.ds(0, (i + 1) * chunk)]

    def hand_on(i, source):
        for e, (live, device) in enumerate(tree):
            @pl.when(live)
            def _():
                remote(part(source, i), part(pivot, i), pivot_send.at[e, i], pivot_recv.at[i], device).start()

    @pl.when(root)
    def _():
        for i in range(4):
            hand_on(i, window)

    @pl.when(c == 0)
    def _():
        for k in range(1, cols):
            remote(window.at[pl.ds(0, TILE), :], top, top_send.at[k], top_recv, (f, r, k)).start()

    def ship(k):
        g = lax.rem(me + k, groups)
        return remote(outgoing.at[g], incoming.at[me], send.at[k], recv.at[k], (g // rows, lax.rem(g, rows), c))

    def land(k):
        g = lax.rem(me + groups - k, groups)
        return remote(outgoing.at[g], incoming.at[g], send.at[k], recv.at[k], (g // rows, lax.rem(g, rows), c))

    def start(k, carry):
        ship(k).start()
        return carry

    lax.fori_loop(1, groups, start, 0)
    own = pltpu.make_async_copy(outgoing.at[me], incoming.at[me], local.at[0])
    own.start()

    @pl.when(root)
    def _():
        for i in range(4):
            copy = pltpu.make_async_copy(part(window, i), part(pivot, i), local.at[1 + i])
            copy.start()
        for i in range(4):
            pltpu.make_async_copy(part(window, i), part(pivot, i), local.at[1 + i]).wait()

    @pl.when(jnp.logical_not(root))
    def _():
        for i in range(4):
            remote(part(window, i), part(pivot, i), pivot_send.at[0, i], pivot_recv.at[i], (f, 0, 0)).wait_recv()
            hand_on(i, pivot)

    symmetric(pivot, a)
    for b in range(HALF):
        inverse_row(b, factor_block(b, 0, a, u, inv, ext), u, inv)
    rest[...] = a[HALF * SB :, HALF * SB :]

    def drain(k, carry):
        land(k).wait_recv()
        ship(k).wait_send()
        return carry

    lax.fori_loop(1, groups, drain, 0)
    own.wait()
    for e, (live, device) in enumerate(tree):
        @pl.when(live)
        def _():
            for i in range(4):
                remote(part(window, i), part(pivot, i), pivot_send.at[e, i], pivot_recv.at[i], device).wait_send()

    @pl.when(c == 0)
    def _():
        for k in range(1, cols):
            remote(window.at[pl.ds(0, TILE), :], top, top_send.at[k], top_recv, (f, r, k)).wait_send()

    @pl.when(c > 0)
    def _():
        remote(window.at[pl.ds(0, TILE), :], top, top_send.at[0], top_recv, (f, r, 0)).wait_recv()


def dot(a, b, dims=(((1,), (0,)), ((), ()))):
    return lax.dot_general(a, b, dims, precision=HIGH, preferred_element_type=jnp.float32)


def down(x, k):
    return jnp.broadcast_to(x[k : k + 1, :], x.shape)


def invert_small(block):
    row = lax.broadcasted_iota(jnp.int32, (SUB, SB), 0)
    lane = lax.broadcasted_iota(jnp.int32, (SUB, SB), 1)
    work = jnp.where(lane < SUB, block, (lane == row + 2 * SUB).astype(jnp.float32))
    pivots = jnp.ones((SUB, SB), jnp.float32)
    for g in range(0, SUB, GROUP):
        columns = [jnp.broadcast_to(work[:, g + q : g + q + 1], (SUB, SB)) for q in range(GROUP)]
        for q in range(GROUP):
            k = g + q
            pivot = down(columns[q], k)
            factor = jnp.where(row > k, columns[q] / pivot, 0.0)
            pivots = jnp.where(row == k, pivot, pivots)
            for later in range(q + 1, GROUP):
                columns[later] = columns[later] - factor * down(columns[later], k)
            work = work - factor * down(work, k)
    work = work * lax.rsqrt(pivots)
    return work[:, 2 * SUB : 3 * SUB]


def factor_block(b, first, a, u, inv, ext, hook=None):
    at = (b - first) * SB
    here = b * SB
    row = lax.broadcasted_iota(jnp.int32, (SB, 2 * SB), 0)
    lane = lax.broadcasted_iota(jnp.int32, (SB, 2 * SB), 1)
    ext[:, :SB] = a[at : at + SB, at : at + SB]
    ext[:, SB:] = (row == lane).astype(jnp.float32)[:, :SB]
    steps = SB // SUB

    def step(s, carry):
        if hook is not None:
            hook(s)
        lo = pl.multiple_of(s * SUB, SUB)
        line = ext[pl.ds(lo, SUB), :]
        small = invert_small(pltpu.roll(line[:, :SB], lax.rem(SB - lo, SB), 1))
        new = dot(small, line)
        new = jnp.where(lane[:SUB] < lo, 0.0, new)
        ext[pl.ds(lo, SUB), :] = new
        left = dot(new[:, :SB], new, (((0,), (0,)), ((), ())))
        ext[...] -= jnp.where(row >= lo + SUB, left, 0.0)
        return carry

    lax.fori_loop(0, steps, step, 0)
    diagonal = ext[:, SB:]
    if here + SB < TILE:
        rest = dot(diagonal, a[at : at + SB, at + SB :])
        u[at : at + SB, here + SB :] = rest
        a[at + SB :, at + SB :] -= dot(rest, rest, (((0,), (0,)), ((), ())))
    return diagonal


def inverse_row(b, diagonal, u, inv):
    here = b * SB
    inv[here : here + SB, :] = jnp.zeros((SB, TILE), jnp.float32)
    inv[here : here + SB, here : here + SB] = diagonal
    if b:
        below = dot(u[:here, here : here + SB], inv[:here, :here], (((0,), (0,)), ((), ())))
        inv[here : here + SB, :here] = -dot(diagonal, below)


def symmetric(pivot, a):
    for i in range(TILE // SB):
        for j in range(i + 1):
            piece = pivot[i * SB : (i + 1) * SB, j * SB : (j + 1) * SB].astype(jnp.float32)
            a[i * SB : (i + 1) * SB, j * SB : (j + 1) * SB] = piece
            if i > j:
                a[j * SB : (j + 1) * SB, i * SB : (i + 1) * SB] = piece.T


def assemble_kernel(marks, window, incoming, acc, bottom):
    groups = incoming.shape[0]
    side = TILE // SB
    acc[...] = window[TILE:, :].astype(jnp.float32)

    def add(p, carry):
        mark = marks[p]

        @pl.when(mark > 0)
        def _():
            slot = mark - 1
            high = pl.ds(pl.multiple_of(slot // side * SB, SB), SB)
            wide = pl.ds(pl.multiple_of(slot % side * SB, SB), SB)
            block = incoming[p // CAP, pl.ds(pl.multiple_of(p % CAP * SB, SB), SB), :]
            acc[high, wide] += block.astype(jnp.float32)

        return carry

    lax.fori_loop(0, groups * CAP, add, 0)
    bottom[...] = acc[...].astype(jnp.bfloat16)


def times(a, b):
    return lax.dot_general(a, b, (((1,), (1,)), ((), ())), preferred_element_type=jnp.float32)


def halves(x):
    high = x.astype(jnp.bfloat16)
    return high, (x - high.astype(jnp.float32)).astype(jnp.bfloat16)


def finish_kernel(
    rows, cols, pattern, window, top, acc, bottom, rest, first_u, first_inv, out, panel, partner, mate, a, u, inv, ext,
    panel_send, panel_recv, mate_send, mate_recv,
):
    f, r, c = lax.axis_index("front"), lax.axis_index("row"), lax.axis_index("col")
    tiles = window.shape[0] // TILE
    owner, within = c // tiles, lax.rem(c, tiles)
    rel = lax.rem(r - owner + rows, rows)
    chunk = TILE // 4
    tree = row_tree(f, rel, owner, c, rows)
    parent = row_parent(f, rel, owner, c, rows)

    barrier = pltpu.get_barrier_semaphore()
    for k in range(1, cols):
        pl.semaphore_signal(barrier, inc=1, device_id=(f, r, lax.rem(c + k, cols)), device_id_type=MESH)
    for k in range(1, rows):
        pl.semaphore_signal(barrier, inc=1, device_id=(f, lax.rem(r + k, rows), c), device_id_type=MESH)
    pl.semaphore_wait(barrier, rows - 1 + cols - 1)

    def rows_of(ref, i):
        return ref.at[pl.ds(i * chunk, chunk), :]

    def send_panel(k, i):
        return remote(rows_of(bottom, i), rows_of(panel, i), panel_send.at[k, i], panel_recv.at[i], (f, r, k))

    def give(e, device, source, i):
        return remote(rows_of(source, i), rows_of(partner, i), mate_send.at[e, i], mate_recv.at[i], device)

    def hand_on(source, i):
        for e, (live, device) in enumerate(tree):
            @pl.when(live)
            def _():
                give(e, device, source, i).start()

    inner = inner_rows(rows)
    depth = jnp.where(rel == 0, 0, 1 + rel // inner)
    deepest = 1 + (rows - 1) // inner

    def pass_on(h):
        i = h - 1 - depth

        @pl.when((c > 0) & (i >= 0) & (i < 4))
        def _():
            here = pl.ds(pl.multiple_of(i * chunk, chunk), chunk)

            @pl.when(rel == 0)
            def _():
                send_panel(0, i).wait_recv()

                @pl.when(within != 0)
                def _():
                    partner[here, :] = panel[here, :]

                @pl.when(within == 0)
                def _():
                    partner[here, :] = top[here, :]

            @pl.when(rel > 0)
            def _():
                give(0, parent, partner, i).wait_recv()

            hand_on(partner, i)

    @pl.when(c == 0)
    def _():
        for i in range(4):
            for k in range(1, cols):
                send_panel(k, i).start()

    cut = HALF * SB
    a[...] = rest[...]
    u[:cut, :] = first_u[...]
    inv[:cut, :] = first_inv[...]
    for b in range(HALF, TILE // SB):
        base = (b - HALF) * 4
        low = u.at[cut:, :]
        diagonal = factor_block(b, HALF, a, low, inv, ext, lambda s: pass_on(base + s))
        inverse_row(b, diagonal, u, inv)
    high, low = halves(inv[...])

    @pl.when(c == 0)
    def _():
        head = window[:TILE, :]
        out[:TILE, :] = (times(head, high) + times(head, low)).astype(jnp.bfloat16)
        for t in range(1, tiles):
            one, two = halves(acc[(t - 1) * TILE : t * TILE, :])
            out[t * TILE : (t + 1) * TILE, :] = (
                times(one, high) + (times(one, low) + times(two, high))
            ).astype(jnp.bfloat16)
        for i in range(4):
            for k in range(1, cols):
                send_panel(k, i).wait_send()

    def later(h, carry):
        pass_on(h)
        return carry

    lax.fori_loop((TILE // SB - HALF) * 4, deepest + 5, later, 0)

    @pl.when(c > 0)
    def _():
        @pl.when(rel > 0)
        def _():
            for i in range(4):
                send_panel(0, i).wait_recv()

        mate[...] = (times(partner[...], high) + times(partner[...], low)).astype(jnp.bfloat16)
        for t in range(tiles):
            source = top[...] if t == 0 else panel[(t - 1) * TILE : t * TILE, :]
            lower = (times(source, high) + times(source, low)).astype(jnp.bfloat16)
            product = times(lower, mate[...])
            base = window[:TILE, :].astype(jnp.float32) if t == 0 else acc[(t - 1) * TILE : t * TILE, :]
            live = pattern[t].astype(jnp.float32)
            out[t * TILE : (t + 1) * TILE, :] = (base - live * product).astype(jnp.bfloat16)
        for e, (live, device) in enumerate(tree):
            @pl.when(live)
            def _():
                for i in range(4):
                    give(e, device, partner, i).wait_send()


def spec(space):
    return pl.BlockSpec(memory_space=space)


def shards(window, children, routes, slots, pattern):
    fronts, rows, cols = lax.axis_size("front"), lax.axis_size("row"), lax.axis_size("col")
    groups = fronts * rows
    count = children.shape[0]
    window = window[0]
    height = window.shape[0]
    target = routes[:, 0]
    earlier = (lax.broadcasted_iota(jnp.int32, (count, count), 0) > lax.broadcasted_iota(jnp.int32, (count, count), 1))
    rank = jnp.sum((earlier & (target[:, None] == target[None, :])).astype(jnp.int32), axis=1)
    place = target * CAP + rank
    hit = lax.broadcasted_iota(jnp.int32, (groups * CAP, count), 0) == place[None, :]
    index = jnp.sum(jnp.where(hit, lax.broadcasted_iota(jnp.int32, hit.shape, 1), 0), axis=1)
    tag = jnp.sum(jnp.where(hit, slots[None, :] + 1, 0), axis=1)
    tagrows = jnp.zeros((groups, 16, SB), jnp.float32) + jnp.pad(
        tag.reshape(groups, CAP).astype(jnp.float32), ((0, 0), (0, SB - CAP))
    )[:, None, :]
    tagrows = tagrows.astype(jnp.bfloat16)
    deep = CAP * SB + 16
    edges = cols - 1 + inner_rows(rows)
    vmem, smem, hbm = pltpu.VMEM, pltpu.SMEM, pl.ANY
    dma = pltpu.SemaphoreType.DMA
    cut = HALF * SB
    f32, bf16 = jnp.float32, jnp.bfloat16
    incoming, top, rest, u, inv = pl.pallas_call(
        functools.partial(exchange_kernel, fronts, rows, cols),
        out_shape=(
            jax.ShapeDtypeStruct((groups, deep, SB), bf16),
            jax.ShapeDtypeStruct((TILE, TILE), bf16),
            jax.ShapeDtypeStruct((TILE - cut, TILE - cut), f32),
            jax.ShapeDtypeStruct((cut, TILE), f32),
            jax.ShapeDtypeStruct((cut, TILE), f32),
        ),
        in_specs=[spec(smem), spec(vmem), spec(vmem), spec(hbm)],
        out_specs=(spec(hbm), spec(hbm), spec(vmem), spec(vmem), spec(vmem)),
        scratch_shapes=[
            vmem((TILE, TILE), bf16), vmem((TILE, TILE), f32), vmem((SB, 2 * SB), f32),
            vmem((groups, deep, SB), bf16),
            dma((groups,)), dma((groups,)), dma((edges, 4)), dma((4,)), dma((cols,)), dma(()), dma((5,)),
        ],
        compiler_params=pltpu.CompilerParams(
            collective_id=0, has_side_effects=True, vmem_limit_bytes=40 << 20
        ),
    )(index, tagrows, children, window)
    marks = incoming[:, CAP * SB, :CAP].astype(jnp.int32).reshape(groups * CAP)
    acc, bottom = pl.pallas_call(
        assemble_kernel,
        out_shape=(
            jax.ShapeDtypeStruct((height - TILE, TILE), f32),
            jax.ShapeDtypeStruct((height - TILE, TILE), bf16),
        ),
        in_specs=[spec(smem), spec(vmem), spec(vmem)],
        out_specs=(spec(vmem),) * 2,
        compiler_params=pltpu.CompilerParams(vmem_limit_bytes=40 << 20),
    )(marks, window, incoming)
    result = pl.pallas_call(
        functools.partial(finish_kernel, rows, cols),
        out_shape=jax.ShapeDtypeStruct((height, TILE), bf16),
        in_specs=[spec(smem)] + [spec(vmem)] * 7,
        out_specs=spec(vmem),
        scratch_shapes=[
            vmem((TILE, TILE), bf16), vmem((TILE, TILE), bf16), vmem((TILE, TILE), bf16),
            vmem((TILE - cut, TILE - cut), f32), vmem((TILE, TILE), f32), vmem((TILE, TILE), f32),
            vmem((SB, 2 * SB), f32),
            dma((cols, 4)), dma((4,)), dma((inner_rows(rows), 4)), dma((4,)),
        ],
        compiler_params=pltpu.CompilerParams(
            collective_id=1, has_side_effects=True, vmem_limit_bytes=40 << 20
        ),
    )(pattern[0, :, 0], window, top, acc, bottom, rest, u, inv)
    return result[None]


def solution(mesh):
    placed = (
        P("front", "row", "col"),
        P(("front", "row", "col"), None, None),
        P(("front", "row", "col"), None),
        P(("front", "row", "col")),
        P("front", "row", "col"),
    )
    return jax.shard_map(
        shards, mesh=mesh, in_specs=placed, out_specs=P("front", "row", "col"), check_vma=False
    )
```

```python
import functools

import jax
import jax.numpy as jnp
from jax import lax
from jax.experimental import pallas as pl
from jax.experimental.pallas import tpu as pltpu
from jax.sharding import PartitionSpec as P

TILE = 512
SB = 128
CAP = 2
SUB = 32
GROUP = 8
HALF = 2
PARTS = 8
MESH = pl.DeviceIdType.MESH
HIGH = lax.Precision.HIGHEST


def inner_rows(rows):
    inner = 1
    while inner * inner * 4 <= rows:
        inner *= 2
    return inner


def row_tree(f, rel, base, c, rows):
    inner = inner_rows(rows)
    edges = []
    for k in range(1, inner):
        edges.append((rel == 0, (f, lax.rem(base + k, rows), c)))
    edges.append((rel + inner < rows, (f, lax.rem(base + rel + inner, rows), c)))
    return edges


def row_parent(f, rel, base, c, rows):
    inner = inner_rows(rows)
    up = jnp.where(rel < inner, 0, rel - inner)
    return (f, lax.rem(base + up, rows), c)


def remote(src, dst, send, recv, device):
    return pltpu.make_async_remote_copy(
        src_ref=src, dst_ref=dst, send_sem=send, recv_sem=recv, device_id=device, device_id_type=MESH
    )


def exchange_kernel(
    fronts, rows, cols, index, tagrows, children, window, incoming, top, rest, u, inv, pivot, a, ext, held, outgoing,
    send, recv, pivot_send, pivot_recv, top_send, top_recv, local,
):
    f, r, c = lax.axis_index("front"), lax.axis_index("row"), lax.axis_index("col")
    groups = fronts * rows
    me = f * rows + r
    chunk = TILE // PARTS
    inner = inner_rows(rows)
    tree = [((r == 0) & (c == 0), (f, 0, k)) for k in range(1, cols)] + row_tree(f, r, 0, c, rows)
    root = (r == 0) & (c == 0)

    fetch = pltpu.make_async_copy(children, held, local.at[PARTS + 1])
    fetch.start()
    barrier = pltpu.get_barrier_semaphore()

    def greet(k, carry):
        g = lax.rem(me + k, groups)
        pl.semaphore_signal(barrier, inc=1, device_id=(g // rows, lax.rem(g, rows), c), device_id_type=MESH)
        return carry

    lax.fori_loop(1, groups, greet, 0)
    for k in range(1, cols):
        pl.semaphore_signal(barrier, inc=1, device_id=(f, r, lax.rem(c + k, cols)), device_id_type=MESH)

    pl.semaphore_wait(barrier, groups - 1 + cols - 1)

    def part(ref, i):
        return ref.at[pl.ds(i * chunk, chunk), pl.ds(0, (i * chunk // SB + 1) * SB)]

    def hand_on(i, source):
        for e, (live, device) in enumerate(tree):
            @pl.when(live)
            def _():
                remote(part(source, i), part(pivot, i), pivot_send.at[e, i], pivot_recv.at[i], device).start()

    @pl.when(root)
    def _():
        for i in range(PARTS):
            hand_on(i, window)

    fetch.wait()

    def pack(g, carry):
        for j in range(CAP):
            outgoing[g, j * SB : (j + 1) * SB, :] = held[index[g * CAP + j]]
        outgoing[g, CAP * SB :, :] = tagrows[g]
        return carry

    lax.fori_loop(0, groups, pack, 0)

    def ship(k):
        g = lax.rem(me + k, groups)
        return remote(outgoing.at[g], incoming.at[me], send.at[k], recv.at[k], (g // rows, lax.rem(g, rows), c))

    def land(k):
        g = lax.rem(me + groups - k, groups)
        return remote(outgoing.at[g], incoming.at[g], send.at[k], recv.at[k], (g // rows, lax.rem(g, rows), c))

    def start(wanted):
        def body(k, carry):
            g = lax.rem(me + k, groups)

            @pl.when(wanted(lax.rem(g, rows) // inner - r // inner))
            def _():
                ship(k).start()

            return carry

        lax.fori_loop(1, groups, body, 0)

    start(lambda up: up <= 0)
    own = pltpu.make_async_copy(outgoing.at[me], incoming.at[me], local.at[0])
    own.start()

    @pl.when(root)
    def _():
        for i in range(PARTS):
            copy = pltpu.make_async_copy(part(window, i), part(pivot, i), local.at[1 + i])
            copy.start()
        for i in range(PARTS):
            pltpu.make_async_copy(part(window, i), part(pivot, i), local.at[1 + i]).wait()

    @pl.when(jnp.logical_not(root))
    def _():
        for i in range(PARTS):
            remote(part(window, i), part(pivot, i), pivot_send.at[0, i], pivot_recv.at[i], (f, 0, 0)).wait_recv()
            hand_on(i, pivot)

    for far in range(1, rows // inner):
        start(lambda up, far=far: up == far)

    @pl.when(c == 0)
    def _():
        for k in range(1, cols):
            remote(window.at[pl.ds(0, TILE), :], top, top_send.at[k], top_recv, (f, r, k)).start()

    symmetric(pivot, a)
    for b in range(HALF):
        inverse_row(b, factor_block(b, 0, a, u, inv, ext), u, inv)
    rest[...] = a[HALF * SB :, HALF * SB :]

    def drain(k, carry):
        land(k).wait_recv()
        ship(k).wait_send()
        return carry

    lax.fori_loop(1, groups, drain, 0)
    own.wait()
    for e, (live, device) in enumerate(tree):
        @pl.when(live)
        def _():
            for i in range(PARTS):
                remote(part(window, i), part(pivot, i), pivot_send.at[e, i], pivot_recv.at[i], device).wait_send()

    @pl.when(c == 0)
    def _():
        for k in range(1, cols):
            remote(window.at[pl.ds(0, TILE), :], top, top_send.at[k], top_recv, (f, r, k)).wait_send()

    @pl.when(c > 0)
    def _():
        remote(window.at[pl.ds(0, TILE), :], top, top_send.at[0], top_recv, (f, r, 0)).wait_recv()


def dot(a, b, dims=(((1,), (0,)), ((), ()))):
    return lax.dot_general(a, b, dims, precision=HIGH, preferred_element_type=jnp.float32)


def down(x, k):
    return jnp.broadcast_to(x[k : k + 1, :], x.shape)


def invert_small(block):
    row = lax.broadcasted_iota(jnp.int32, (SUB, SB), 0)
    lane = lax.broadcasted_iota(jnp.int32, (SUB, SB), 1)
    work = jnp.where(lane < SUB, block, (lane == row + 2 * SUB).astype(jnp.float32))
    pivots = jnp.ones((SUB, SB), jnp.float32)
    for g in range(0, SUB, GROUP):
        columns = [jnp.broadcast_to(work[:, g + q : g + q + 1], (SUB, SB)) for q in range(GROUP)]
        for q in range(GROUP):
            k = g + q
            pivot = down(columns[q], k)
            factor = jnp.where(row > k, columns[q] / pivot, 0.0)
            pivots = jnp.where(row == k, pivot, pivots)
            for later in range(q + 1, GROUP):
                columns[later] = columns[later] - factor * down(columns[later], k)
            work = work - factor * down(work, k)
    work = work * lax.rsqrt(pivots)
    return work[:, 2 * SUB : 3 * SUB]


def factor_block(b, first, a, u, inv, ext, hook=None):
    at = (b - first) * SB
    here = b * SB
    row = lax.broadcasted_iota(jnp.int32, (SB, 2 * SB), 0)
    lane = lax.broadcasted_iota(jnp.int32, (SB, 2 * SB), 1)
    ext[:, :SB] = a[at : at + SB, at : at + SB]
    ext[:, SB:] = (row == lane).astype(jnp.float32)[:, :SB]
    steps = SB // SUB

    def step(s, carry):
        if hook is not None:
            hook(s)
        lo = pl.multiple_of(s * SUB, SUB)
        line = ext[pl.ds(lo, SUB), :]
        small = invert_small(pltpu.roll(line[:, :SB], lax.rem(SB - lo, SB), 1))
        new = dot(small, line)
        new = jnp.where(lane[:SUB] < lo, 0.0, new)
        ext[pl.ds(lo, SUB), :] = new
        left = dot(new[:, :SB], new, (((0,), (0,)), ((), ())))
        ext[...] -= jnp.where(row >= lo + SUB, left, 0.0)
        return carry

    lax.fori_loop(0, steps, step, 0)
    diagonal = ext[:, SB:]
    if here + SB < TILE:
        rest = dot(diagonal, a[at : at + SB, at + SB :])
        u[at : at + SB, here + SB :] = rest
        a[at + SB :, at + SB :] -= dot(rest, rest, (((0,), (0,)), ((), ())))
    return diagonal


def inverse_row(b, diagonal, u, inv):
    here = b * SB
    inv[here : here + SB, :] = jnp.zeros((SB, TILE), jnp.float32)
    inv[here : here + SB, here : here + SB] = diagonal
    if b:
        below = dot(u[:here, here : here + SB], inv[:here, :here], (((0,), (0,)), ((), ())))
        inv[here : here + SB, :here] = -dot(diagonal, below)


def symmetric(pivot, a):
    for i in range(TILE // SB):
        for j in range(i + 1):
            piece = pivot[i * SB : (i + 1) * SB, j * SB : (j + 1) * SB].astype(jnp.float32)
            a[i * SB : (i + 1) * SB, j * SB : (j + 1) * SB] = piece
            if i > j:
                a[j * SB : (j + 1) * SB, i * SB : (i + 1) * SB] = piece.T


def assemble_kernel(marks, window, incoming, acc, bottom):
    groups = incoming.shape[0]
    side = TILE // SB
    acc[...] = window[TILE:, :].astype(jnp.float32)

    def add(p, carry):
        mark = marks[p]

        @pl.when(mark > 0)
        def _():
            slot = mark - 1
            high = pl.ds(pl.multiple_of(slot // side * SB, SB), SB)
            wide = pl.ds(pl.multiple_of(slot % side * SB, SB), SB)
            block = incoming[p // CAP, pl.ds(pl.multiple_of(p % CAP * SB, SB), SB), :]
            acc[high, wide] += block.astype(jnp.float32)

        return carry

    lax.fori_loop(0, groups * CAP, add, 0)
    bottom[...] = acc[...].astype(jnp.bfloat16)


def times(a, b):
    return lax.dot_general(a, b, (((1,), (1,)), ((), ())), preferred_element_type=jnp.float32)


def halves(x):
    high = x.astype(jnp.bfloat16)
    return high, (x - high.astype(jnp.float32)).astype(jnp.bfloat16)


def finish_kernel(
    rows, cols, pattern, window, top, acc, bottom, rest, first_u, first_inv, out, panel, partner, mate, lower, a, u, inv, ext,
    panel_send, panel_recv, mate_send, mate_recv,
):
    f, r, c = lax.axis_index("front"), lax.axis_index("row"), lax.axis_index("col")
    tiles = window.shape[0] // TILE
    owner, within = c // tiles, lax.rem(c, tiles)
    rel = lax.rem(r - owner + rows, rows)
    chunk = TILE // PARTS
    tree = row_tree(f, rel, owner, c, rows)
    parent = row_parent(f, rel, owner, c, rows)

    barrier = pltpu.get_barrier_semaphore()
    for k in range(1, cols):
        pl.semaphore_signal(barrier, inc=1, device_id=(f, r, lax.rem(c + k, cols)), device_id_type=MESH)
    for k in range(1, rows):
        pl.semaphore_signal(barrier, inc=1, device_id=(f, lax.rem(r + k, rows), c), device_id_type=MESH)
    pl.semaphore_wait(barrier, rows - 1 + cols - 1)

    def rows_of(ref, i):
        return ref.at[pl.ds(i * chunk, chunk), :]

    def send_panel(k, i):
        return remote(rows_of(bottom, i), rows_of(panel, i), panel_send.at[k, i], panel_recv.at[i], (f, r, k))

    def give(e, device, source, i):
        return remote(rows_of(source, i), rows_of(partner, i), mate_send.at[e, i], mate_recv.at[i], device)

    def hand_on(source, i):
        for e, (live, device) in enumerate(tree):
            @pl.when(live)
            def _():
                give(e, device, source, i).start()

    inner = inner_rows(rows)
    depth = jnp.where(rel == 0, 0, 1 + rel // inner)
    deepest = 1 + (rows - 1) // inner

    def pass_on(h):
        i = h - 1 - depth

        @pl.when((c > 0) & (i >= 0) & (i < PARTS))
        def _():
            here = pl.ds(pl.multiple_of(i * chunk, chunk), chunk)

            @pl.when(rel == 0)
            def _():
                send_panel(0, i).wait_recv()

                @pl.when(within != 0)
                def _():
                    partner[here, :] = panel[here, :]

                @pl.when(within == 0)
                def _():
                    partner[here, :] = top[here, :]

            @pl.when(rel > 0)
            def _():
                give(0, parent, partner, i).wait_recv()

            hand_on(partner, i)

    @pl.when(c == 0)
    def _():
        for i in range(PARTS):
            for k in range(1, cols):
                send_panel(k, i).start()

    cut = HALF * SB
    a[...] = rest[...]
    u[:cut, :] = first_u[...]
    inv[:cut, :] = first_inv[...]
    for b in range(HALF, TILE // SB):
        base = (b - HALF) * 4
        low = u.at[cut:, :]
        diagonal = factor_block(b, HALF, a, low, inv, ext, lambda s: pass_on(base + s))
        inverse_row(b, diagonal, u, inv)
    high, low = halves(inv[...])

    @pl.when(c == 0)
    def _():
        head = window[:TILE, :]
        out[:TILE, :] = (times(head, high) + times(head, low)).astype(jnp.bfloat16)
        for t in range(1, tiles):
            one, two = halves(acc[(t - 1) * TILE : t * TILE, :])
            out[t * TILE : (t + 1) * TILE, :] = (
                times(one, high) + (times(one, low) + times(two, high))
            ).astype(jnp.bfloat16)
        for i in range(PARTS):
            for k in range(1, cols):
                send_panel(k, i).wait_send()

    def later(h, carry):
        pass_on(h)
        return carry

    done = (TILE // SB - HALF) * 4
    lax.fori_loop(done, done + 3, later, 0)

    @pl.when(c > 0)
    def _():
        lower[:TILE, :] = (times(top[...], high) + times(top[...], low)).astype(jnp.bfloat16)

    lax.fori_loop(done + 3, max(deepest + PARTS + 1, done + 3), later, 0)

    @pl.when(c > 0)
    def _():
        @pl.when(rel > 0)
        def _():
            for i in range(PARTS):
                send_panel(0, i).wait_recv()

        mate[...] = (times(partner[...], high) + times(partner[...], low)).astype(jnp.bfloat16)
        for t in range(tiles):
            if t:
                source = panel[(t - 1) * TILE : t * TILE, :]
                lower[t * TILE : (t + 1) * TILE, :] = (times(source, high) + times(source, low)).astype(jnp.bfloat16)
            product = times(lower[t * TILE : (t + 1) * TILE, :], mate[...])
            base = window[:TILE, :].astype(jnp.float32) if t == 0 else acc[(t - 1) * TILE : t * TILE, :]
            live = pattern[t].astype(jnp.float32)
            out[t * TILE : (t + 1) * TILE, :] = (base - live * product).astype(jnp.bfloat16)
        for e, (live, device) in enumerate(tree):
            @pl.when(live)
            def _():
                for i in range(PARTS):
                    give(e, device, partner, i).wait_send()


def spec(space):
    return pl.BlockSpec(memory_space=space)


def shards(window, children, routes, slots, pattern):
    fronts, rows, cols = lax.axis_size("front"), lax.axis_size("row"), lax.axis_size("col")
    groups = fronts * rows
    count = children.shape[0]
    window = window[0]
    height = window.shape[0]
    target = routes[:, 0]
    earlier = (lax.broadcasted_iota(jnp.int32, (count, count), 0) > lax.broadcasted_iota(jnp.int32, (count, count), 1))
    rank = jnp.sum((earlier & (target[:, None] == target[None, :])).astype(jnp.int32), axis=1)
    place = target * CAP + rank
    hit = lax.broadcasted_iota(jnp.int32, (groups * CAP, count), 0) == place[None, :]
    index = jnp.sum(jnp.where(hit, lax.broadcasted_iota(jnp.int32, hit.shape, 1), 0), axis=1)
    tag = jnp.sum(jnp.where(hit, slots[None, :] + 1, 0), axis=1)
    tagrows = jnp.zeros((groups, 16, SB), jnp.float32) + jnp.pad(
        tag.reshape(groups, CAP).astype(jnp.float32), ((0, 0), (0, SB - CAP))
    )[:, None, :]
    tagrows = tagrows.astype(jnp.bfloat16)
    deep = CAP * SB + 16
    edges = cols - 1 + inner_rows(rows)
    vmem, smem, hbm = pltpu.VMEM, pltpu.SMEM, pl.ANY
    dma = pltpu.SemaphoreType.DMA
    cut = HALF * SB
    f32, bf16 = jnp.float32, jnp.bfloat16
    incoming, top, rest, u, inv = pl.pallas_call(
        functools.partial(exchange_kernel, fronts, rows, cols),
        out_shape=(
            jax.ShapeDtypeStruct((groups, deep, SB), bf16),
            jax.ShapeDtypeStruct((TILE, TILE), bf16),
            jax.ShapeDtypeStruct((TILE - cut, TILE - cut), f32),
            jax.ShapeDtypeStruct((cut, TILE), f32),
            jax.ShapeDtypeStruct((cut, TILE), f32),
        ),
        in_specs=[spec(smem), spec(vmem), spec(hbm), spec(hbm)],
        out_specs=(spec(hbm), spec(hbm), spec(vmem), spec(vmem), spec(vmem)),
        scratch_shapes=[
            vmem((TILE, TILE), bf16), vmem((TILE, TILE), f32), vmem((SB, 2 * SB), f32),
            vmem((count, SB, SB), bf16), vmem((groups, deep, SB), bf16),
            dma((groups,)), dma((groups,)), dma((edges, PARTS)), dma((PARTS,)), dma((cols,)), dma(()), dma((PARTS + 2,)),
        ],
        compiler_params=pltpu.CompilerParams(
            collective_id=0, has_side_effects=True, vmem_limit_bytes=40 << 20
        ),
    )(index, tagrows, children, window)
    marks = incoming[:, CAP * SB, :CAP].astype(jnp.int32).reshape(groups * CAP)
    acc, bottom = pl.pallas_call(
        assemble_kernel,
        out_shape=(
            jax.ShapeDtypeStruct((height - TILE, TILE), f32),
            jax.ShapeDtypeStruct((height - TILE, TILE), bf16),
        ),
        in_specs=[spec(smem), spec(vmem), spec(vmem)],
        out_specs=(spec(vmem),) * 2,
        compiler_params=pltpu.CompilerParams(vmem_limit_bytes=40 << 20),
    )(marks, window, incoming)
    result = pl.pallas_call(
        functools.partial(finish_kernel, rows, cols),
        out_shape=jax.ShapeDtypeStruct((height, TILE), bf16),
        in_specs=[spec(smem)] + [spec(vmem)] * 7,
        out_specs=spec(vmem),
        scratch_shapes=[
            vmem((TILE, TILE), bf16), vmem((TILE, TILE), bf16), vmem((TILE, TILE), bf16), vmem((height, TILE), bf16),
            vmem((TILE - cut, TILE - cut), f32), vmem((TILE, TILE), f32), vmem((TILE, TILE), f32),
            vmem((SB, 2 * SB), f32),
            dma((cols, PARTS)), dma((PARTS,)), dma((inner_rows(rows), PARTS)), dma((PARTS,)),
        ],
        compiler_params=pltpu.CompilerParams(
            collective_id=1, has_side_effects=True, vmem_limit_bytes=40 << 20
        ),
    )(pattern[0, :, 0], window, top, acc, bottom, rest, u, inv)
    return result[None]


def solution(mesh):
    placed = (
        P("front", "row", "col"),
        P(("front", "row", "col"), None, None),
        P(("front", "row", "col"), None),
        P(("front", "row", "col")),
        P("front", "row", "col"),
    )
    return jax.shard_map(
        shards, mesh=mesh, in_specs=placed, out_specs=P("front", "row", "col"), check_vma=False
    )
```
